128 devices in a mesh: row: 16 (over z, y), col: 8 (over x, core).
Axes of the slice: x: 4, y: 4, z: 4, core: 2. Of those that a mesh axis runs over, the one named last changes fastest.
Arguments:
- tokens: bfloat16 [2048, 8192], P('row', 'col'), may hold values from -6 to 6
- w_gate: bfloat16 [8192, 14336], P('col', 'row'), may hold values from -0.0625 to 0.0625
- w_up: bfloat16 [8192, 14336], P('col', 'row'), may hold values from -0.0625 to 0.0625
- w_down: bfloat16 [14336, 8192], P('row', 'col'), may hold values from -0.046875 to 0.046875
- cotangent: bfloat16 [2048, 8192], P('row', 'col'), may hold values from -0.3125 to 0.3125
Outputs:
- mixed: bfloat16 [2048, 8192], P('row', 'col')
- grad_gate: bfloat16 [8192, 14336], P('col', 'row')
- grad_up: bfloat16 [8192, 14336], P('col', 'row')
- grad_down: bfloat16 [14336, 8192], P('row', 'col')
The draws below stay inside these ranges and needn't reach their ends.
All inputs are finite; a program needn't handle non-finite values.
Results may differ from the reference program's by a relative error of at most 0.04.
Values may be sent and summed in bfloat16 or wider, within the bound.
No kernel may reach another device: no remote copies, remote signals or barrier semaphores. Data moves between devices by JAX's collectives and lax.ppermute only.
A program may use at most 128 MiB of HBM per device.

```python
import jax
import jax.numpy as jnp
from jax import lax

D = 8192
FF = 14336
TOKENS = 2048
N_COL = 8


def level_of(own_key, shape, shards, low, high):
    loudness = 1.0
    for position, shards_of in shards:
        draws = jax.random.uniform(jax.random.fold_in(jax.random.fold_in(own_key, 6), position), (shards_of,), jnp.float32, low / len(shards), high / len(shards))
        loudness = loudness * jnp.repeat(jnp.exp(draws), shape[position] // shards_of).reshape((-1,) + (1,) * (len(shape) - 1 - position))
    return loudness


def noise(key, shape, deviation, limit, pieces=(), dtype=jnp.bfloat16):
    level = level_of(key, shape, pieces, -0.22, 0.18) if pieces else 1.0
    values = jax.random.normal(key, shape, jnp.float32) * deviation * level
    return jnp.minimum(jnp.maximum(values, -limit), limit).astype(dtype)


def setup_inputs(seed: int = 0) -> dict:
    splits = jax.random.split(jax.random.key(seed), 6)
    return {
        "tokens": noise(splits[0], (TOKENS, D), 1.0, 6.0, ((0, 16), (1, 8))),
        "w_gate": noise(splits[1], (D, FF), D ** -0.5, 0.0625, ((0, 8), (1, 16))),
        "w_up": noise(splits[2], (D, FF), D ** -0.5, 0.0625, ((0, 8), (1, 16))),
        "w_down": noise(splits[3], (FF, D), FF ** -0.5, 0.046875, ((0, 16), (1, 8))),
        "cotangent": noise(splits[4], (TOKENS, D), (TOKENS ** -0.5), 0.3125, ((0, 16), (1, 8))),
    }


def blocked_sum(left, right_t):
    block = left.shape[1] // N_COL
    total = jnp.zeros((left.shape[0], right_t.shape[0]), jnp.float32)
    for index in range(N_COL):
        piece_left = left[:, index * block:(index + 1) * block]
        piece_right = right_t[:, index * block:(index + 1) * block]
        term = jnp.dot(piece_left, piece_right.T, preferred_element_type=jnp.float32)
        rounded = lax.optimization_barrier(term.astype(jnp.bfloat16))
        total = total + rounded.astype(jnp.float32)
    return total


def reference(tokens, w_gate, w_up, w_down, cotangent):
    gate_sum = blocked_sum(tokens, w_gate.T)
    up_sum = blocked_sum(tokens, w_up.T)
    sigmoid_gate = jax.nn.sigmoid(gate_sum)
    silu_gate = gate_sum * sigmoid_gate
    hidden = (silu_gate * up_sum).astype(jnp.bfloat16)
    mixed = jnp.dot(hidden, w_down, preferred_element_type=jnp.float32).astype(jnp.bfloat16)
    grad_down = jnp.dot(hidden.T, cotangent, preferred_element_type=jnp.float32).astype(jnp.bfloat16)
    hidden_grad = blocked_sum(cotangent, w_down)
    pre_gate = (hidden_grad * up_sum * sigmoid_gate * (1.0 + gate_sum * (1.0 - sigmoid_gate))).astype(jnp.bfloat16)
    pre_up = (hidden_grad * silu_gate).astype(jnp.bfloat16)
    grad_gate = jnp.dot(tokens.T, pre_gate, preferred_element_type=jnp.float32).astype(jnp.bfloat16)
    grad_up = jnp.dot(tokens.T, pre_up, preferred_element_type=jnp.float32).astype(jnp.bfloat16)
    return mixed, grad_gate, grad_up, grad_down
```

```python
import jax
import jax.numpy as jnp
from jax import lax
from jax.sharding import PartitionSpec as P

RING = 4
CORES = 2
AXES = ("row", "col")
GATE_GROUPS = ((0,), (1, 3), (2,))
GRAD_GROUPS = ((0, 1, 3), (2,))


def place(z, y, x, core):
    return ((z * RING + y) * RING + x) * CORES + core


def permute(value, move):
    pairs = []
    for z in range(RING):
        for y in range(RING):
            for x in range(RING):
                for core in range(CORES):
                    target = move(z, y, x, core)
                    pairs.append(
                        (
                            place(z, y, x, core),
                            place(
                                target[0] % RING,
                                target[1] % RING,
                                target[2] % RING,
                                target[3],
                            ),
                        )
                    )
    return lax.ppermute(value, AXES, pairs)


def swap_cores(value):
    return permute(value, lambda z, y, x, core: (z, y, x, 1 - core))


def ring_hop(value):
    return permute(value, lambda z, y, x, core: (z, y, x + 1 - 2 * core, core))


def first_shift(value, by):
    return permute(
        value,
        lambda z, y, x, core: (z, y + by, x, core) if core == 0 else (z + by, y, x, core),
    )


def second_shift(value, by):
    return permute(
        value,
        lambda z, y, x, core: (z + by, y, x, core) if core == 0 else (z, y + by, x, core),
    )


def tie(*values):
    return lax.optimization_barrier(values)


def gather_first(own):
    near = first_shift(own, 1), first_shift(own, 3)
    far = first_shift(own, 2)
    return jnp.concatenate([own, near[1], far, near[0]], axis=0)


def gather_second(own):
    near = second_shift(own, 1), second_shift(own, 3)
    far = second_shift(own, 2)
    return [own, near[1], far, near[0]]


def wide(value):
    return value.astype(jnp.float32)


def narrow(value):
    return value.astype(jnp.bfloat16)


def dot(left, right, dims):
    return lax.dot_general(left, right, (dims, ((), ())), preferred_element_type=jnp.float32)


def gather(slabs, group):
    return slabs[group[0]] if len(group) == 1 else jnp.concatenate([slabs[o] for o in group], axis=0)


def take(partial, index):
    return lax.dynamic_index_in_dim(partial, index % RING, axis=1, keepdims=False)


def ring_sum(partial, rho):
    moving = take(partial, rho + 3)
    for step in range(1, RING):
        moving = ring_hop(moving)
        total = wide(moving) + wide(take(partial, rho + 3 - step))
        if step < RING - 1:
            moving = narrow(total)
    return total


def ring_gather(own, rho):
    slabs, tokens, width = own.shape
    whole = jnp.zeros((slabs, RING, tokens, width), own.dtype)
    moving = own
    for step in range(RING):
        whole = lax.dynamic_update_slice_in_dim(whole, moving[:, None], (rho + RING - step) % RING, axis=1)
        if step < RING - 1:
            moving = ring_hop(moving)
    return whole


def in_order(groups, parts):
    where = {o: (i, j) for i, group in enumerate(groups) for j, o in enumerate(group)}
    return jnp.stack([parts[where[o][0]][where[o][1]] for o in range(RING)], axis=0)


def local(tokens, w_gate, w_up, w_down, cotangent):
    col = lax.axis_index("col")
    core, x = col % CORES, col // CORES
    rho = jnp.where(core == 0, x, (RING - x) % RING)
    rows, features = tokens.shape
    half = rows // CORES
    hidden_width = w_gate.shape[1]

    acts = jnp.stack([tokens, cotangent]).reshape(2, CORES, half, features)
    mine = lax.dynamic_index_in_dim(acts, core, axis=1, keepdims=False)
    theirs = lax.dynamic_index_in_dim(acts, 1 - core, axis=1, keepdims=False)
    acts = jnp.concatenate([mine, swap_cores(theirs)], axis=2)
    joined = jnp.concatenate([w_gate, w_up], axis=1)
    joined = jnp.concatenate([joined, swap_cores(joined)], axis=0)
    down = jnp.concatenate([w_down, swap_cores(w_down)], axis=1)

    token_slabs = gather_second(gather_first(acts[0]))
    cot_own, token_slabs[1], token_slabs[3] = tie(acts[1], token_slabs[1], token_slabs[3])
    cot_slabs = gather_second(gather_first(cot_own))

    sums = []
    for group in GATE_GROUPS:
        partial = narrow(dot(gather(token_slabs, group), joined, ((1,), (0,))))
        sums.append(ring_sum(partial.reshape(len(group), RING, half, 2 * hidden_width), rho))
    sums = in_order(GATE_GROUPS, sums)
    gate_sum, up_sum = sums[..., :hidden_width], sums[..., hidden_width:]
    sigmoid = jax.nn.sigmoid(gate_sum)
    silu = gate_sum * sigmoid
    hidden = ring_gather(narrow(silu * up_sum), rho)
    hidden = hidden.reshape(RING * RING * half, hidden_width)

    sums = []
    for group in GRAD_GROUPS:
        partial = narrow(dot(gather(cot_slabs, group), down, ((1,), (1,))))
        sums.append(ring_sum(partial.reshape(len(group), RING, half, hidden_width), rho))
    hidden_grad = in_order(GRAD_GROUPS, sums)
    pre_gate = narrow(hidden_grad * up_sum * sigmoid * (1.0 + gate_sum * (1.0 - sigmoid)))
    pre_up = narrow(hidden_grad * silu)
    pre_gate = ring_gather(pre_gate, rho).reshape(hidden.shape)
    pre_up = ring_gather(pre_up, rho).reshape(hidden.shape)

    partial = narrow(dot(hidden, down, ((1,), (0,)))).reshape(RING, RING * half, CORES * features)
    slab = wide(partial[0])
    for by in (1, 3, 2):
        slab = slab + wide(second_shift(partial[by], by))
    slab = narrow(slab).reshape(RING, half, CORES * features)
    block = wide(slab[0])
    for by in (1, 3, 2):
        block = block + wide(first_shift(slab[by], by))
    block = narrow(block)
    other = swap_cores(block[:, features:])
    mixed = jnp.zeros((CORES, half, features), jnp.bfloat16)
    mixed = lax.dynamic_update_slice_in_dim(mixed, block[None, :, :features], core, axis=0)
    mixed = lax.dynamic_update_slice_in_dim(mixed, other[None], 1 - core, axis=0)
    mixed = mixed.reshape(rows, features)

    all_tokens = jnp.concatenate(token_slabs, axis=0)
    all_cot = jnp.concatenate(cot_slabs, axis=0)

    def weight_grad(left, right):
        return dot(left, right, ((0,), (0,)))

    sent = swap_cores(narrow(weight_grad(hidden, all_cot[:, features:])))
    grad_down = narrow(weight_grad(hidden, all_cot[:, :features]) + wide(sent))
    sent = swap_cores(narrow(weight_grad(all_tokens[:, features:], pre_gate)))
    grad_gate = narrow(weight_grad(all_tokens[:, :features], pre_gate) + wide(sent))
    sent = swap_cores(narrow(weight_grad(all_tokens[:, features:], pre_up)))
    grad_up = narrow(weight_grad(all_tokens[:, :features], pre_up) + wide(sent))
    return mixed, grad_gate, grad_up, grad_down


def solution(mesh):
    return jax.shard_map(
        local,
        mesh=mesh,
        in_specs=(
            P("row", "col"),
            P("col", "row"),
            P("col", "row"),
            P("row", "col"),
            P("row", "col"),
        ),
        out_specs=(P("row", "col"), P("col", "row"), P("col", "row"), P("row", "col")),
        check_vma=False,
    )
```

```python
import functools

import jax
import jax.numpy as jnp
from jax import lax
from jax.experimental import pallas as pl
from jax.experimental.pallas import tpu as pltpu
from jax.sharding import PartitionSpec as P

RING = 4
CORES = 2
DEPTH_STEPS = 2
AXES = ("row", "col")
LONG = pl.CostEstimate(flops=2 * 10**10, bytes_accessed=1, transcendentals=0)


def place(z, y, x, core):
    return ((z * RING + y) * RING + x) * CORES + core


def permute(value, move, name):
    pairs = []
    for z in range(RING):
        for y in range(RING):
            for x in range(RING):
                for core in range(CORES):
                    target = move(z, y, x, core)
                    pairs.append(
                        (
                            place(z, y, x, core),
                            place(
                                target[0] % RING,
                                target[1] % RING,
                                target[2] % RING,
                                target[3],
                            ),
                        )
                    )
    with jax.named_scope(name):
        return lax.ppermute(value, AXES, pairs)


def swap_cores(value, name):
    return permute(value, lambda z, y, x, core: (z, y, x, 1 - core), name)


def first_shift(value, by, name):
    return permute(
        value,
        lambda z, y, x, core: (z, y + by, x, core) if core == 0 else (z + by, y, x, core),
        name,
    )


def second_shift(value, by, name):
    return permute(
        value,
        lambda z, y, x, core: (z + by, y, x, core) if core == 0 else (z, y + by, x, core),
        name,
    )


def ring_shift(value, name):
    return permute(value, lambda z, y, x, core: (z, y, x + 1 - 2 * core, core), name)


def tie(*values):
    return lax.optimization_barrier(values)


def gather_first(own, name):
    before, after, far = (first_shift(own, by, f"{name}_first_{by}") for by in (1, 3, 2))
    return jnp.concatenate([own, after, far, before], axis=0)


def gather_near(own, name):
    return second_shift(own, 3, f"{name}_near_3"), second_shift(own, 1, f"{name}_near_1")


def gather_far(after, before, name):
    half = before.shape[0] // 2
    return jnp.concatenate(
        [
            second_shift(before[:half], 1, f"{name}_far_1"),
            second_shift(after[half:], 3, f"{name}_far_3"),
        ],
        axis=0,
    )


def sum_second(slabs):
    own, after, far, before = slabs
    half = own.shape[0] // 2
    far_after = second_shift(far[:half], 1, "mixed_far_1")
    far_before = second_shift(far[half:], 3, "mixed_far_3")
    after = jnp.concatenate([narrow(wide(after[:half]) + wide(far_after)), after[half:]], axis=0)
    before = jnp.concatenate([before[:half], narrow(wide(before[half:]) + wide(far_before))], axis=0)
    after = second_shift(after, 1, "mixed_near_1")
    before = second_shift(before, 3, "mixed_near_3")
    return wide(own) + wide(after) + wide(before)


def project_block(count, pairs, *refs):
    own, other = refs[:count], refs[count : 2 * count]
    weights, out_ref, acc = refs[2 * count : -2], refs[-2], refs[-1]
    step = pl.program_id(0)
    left = jnp.concatenate(
        [jnp.concatenate([ref[...] for ref in part], axis=0) for part in (own, other)], axis=1
    )
    width = weights[0].shape[1]
    for pair in range(pairs):
        at = pair * width
        right = jnp.concatenate([weights[2 * pair][...], weights[2 * pair + 1][...]], axis=0)
        term = jnp.dot(left, right, preferred_element_type=jnp.float32)

        @pl.when(step == 0)
        def _():
            acc[:, at : at + width] = term

        @pl.when(step == DEPTH_STEPS - 1)
        def _():
            out_ref[:, at : at + width] = (acc[:, at : at + width] + term).astype(out_ref.dtype)


def in_hbm(weights):
    return [pltpu.with_memory_space_constraint(w, pltpu.HBM) for w in weights]


def project(slabs, *weights):
    count, tokens = len(slabs), slabs[0].shape[0]
    features, width = weights[0].shape
    pairs = len(weights) // 2
    depth = features // DEPTH_STEPS
    own = pl.BlockSpec((tokens, depth), lambda k: (0, k))
    other = pl.BlockSpec((tokens, depth), lambda k: (0, k + DEPTH_STEPS))
    weight = pl.BlockSpec((depth, width), lambda k: (k, 0))
    shape = count * tokens, pairs * width
    return pl.pallas_call(
        functools.partial(project_block, count, pairs),
        grid=(DEPTH_STEPS,),
        in_specs=[own] * count + [other] * count + [weight] * len(weights),
        out_specs=pl.BlockSpec(shape, lambda k: (0, 0)),
        out_shape=jax.ShapeDtypeStruct(shape, jnp.bfloat16),
        scratch_shapes=[pltpu.VMEM(shape, jnp.float32)],
        compiler_params=pltpu.CompilerParams(vmem_limit_bytes=28 * 2**20),
        cost_estimate=LONG,
    )(*slabs, *slabs, *in_hbm(weights))


def down_block(count, *refs):
    own_ref, other_ref, out_ref = refs[count:]
    features = own_ref.shape[1]
    for i in range(count):

        @pl.when(pl.program_id(0) == i)
        def _():
            slab = refs[i][...]
            for at, weight in ((0, own_ref), (features, other_ref)):
                term = jnp.dot(slab, weight[...], preferred_element_type=jnp.float32)
                out_ref[:, at : at + features] = term.astype(out_ref.dtype)


def back_block(count, *refs):
    own_ref, other_ref, out_ref = refs[count:]
    features = own_ref.shape[1]
    dims = (((1,), (1,)), ((), ()))
    for i in range(count):

        @pl.when(pl.program_id(0) == i)
        def _():
            slab = refs[i][...]
            term = lax.dot_general(slab[:, :features], own_ref[...], dims, preferred_element_type=jnp.float32)
            term += lax.dot_general(slab[:, features:], other_ref[...], dims, preferred_element_type=jnp.float32)
            out_ref[...] = term.astype(out_ref.dtype)


def by_slab(block, slabs, own, other, width):
    count, (tokens, depth) = len(slabs), slabs[0].shape
    whole = pl.BlockSpec(own.shape, lambda i: (0, 0))
    return pl.pallas_call(
        functools.partial(block, count),
        grid=(count,),
        in_specs=[pl.BlockSpec((tokens, depth), lambda i: (0, 0))] * count + [whole, whole],
        out_specs=pl.BlockSpec((tokens, width), lambda i: (i, 0)),
        out_shape=jax.ShapeDtypeStruct((count * tokens, width), jnp.bfloat16),
        compiler_params=pltpu.CompilerParams(vmem_limit_bytes=28 * 2**20),
        cost_estimate=LONG,
    )(*slabs, *in_hbm([own, other]))


def wide(value):
    return value.astype(jnp.float32)


def narrow(value):
    return value.astype(jnp.bfloat16)


def dot(left, right, dims):
    return lax.dot_general(left, right, (dims, ((), ())), preferred_element_type=jnp.float32)


def take(partial, index):
    return lax.dynamic_index_in_dim(partial, index % RING, axis=1, keepdims=False)


def sum_hop(partial, moving, rho, step, name):
    moving = ring_shift(narrow(moving), f"{name}_hop{step}")
    return wide(moving) + wide(take(partial, rho + 3 - step))


def assemble(parts, rho):
    slabs, tokens, width = parts[0].shape
    whole = jnp.zeros((slabs, RING, tokens, width), parts[0].dtype)
    for step, part in enumerate(parts):
        whole = lax.dynamic_update_slice_in_dim(
            whole, part[:, None], (rho + RING - step) % RING, axis=1
        )
    return whole


def local(tokens, w_gate, w_up, w_down, cotangent):
    col = lax.axis_index("col")
    core, x = col % CORES, col // CORES
    rho = jnp.where(core == 0, x, (RING - x) % RING)
    rows, features = tokens.shape
    half = rows // CORES
    hidden_width = w_gate.shape[1]

    acts = jnp.stack([tokens, cotangent]).reshape(2, CORES, half, features)
    mine = lax.dynamic_index_in_dim(acts, core, axis=1, keepdims=False)
    theirs = lax.dynamic_index_in_dim(acts, 1 - core, axis=1, keepdims=False)
    theirs = swap_cores(theirs, "acts_swap")
    theirs, w_gate_sent, w_up_sent = tie(theirs, w_gate, w_up)
    acts = jnp.concatenate([mine, theirs], axis=2)
    w_gate_other, w_up_other = swap_cores(w_gate_sent, "gate_swap"), swap_cores(w_up_sent, "up_swap")

    def split(partial):
        return partial.reshape(-1, RING, half, partial.shape[-1])

    tok0 = gather_first(acts[0], "tok")
    tok0, w_gate_other, w_up_other, w_down_sent = tie(tok0, w_gate_other, w_up_other, w_down)
    tok1, tok3 = gather_near(tok0, "tok")
    w_down_other = swap_cores(w_down_sent, "down_swap")
    weights = w_gate, w_gate_other, w_up, w_up_other
    own = split(project([tok0], *weights))
    own, w_down_other = tie(own, w_down_other)
    own_sum = sum_hop(own, take(own, rho + 3), rho, 1, "own")
    cot_own, tok1, tok3, own_sum = tie(acts[1], tok1, tok3, own_sum)
    tok2 = gather_far(tok1, tok3, "tok")
    cot0 = gather_first(cot_own, "cot")
    own_sum = sum_hop(own, own_sum, rho, 2, "own")
    near = split(project([tok1, tok3], *weights))
    near, own_sum = tie(near, own_sum)
    own_sum = sum_hop(own, own_sum, rho, 3, "own")
    near_sum = sum_hop(near, take(near, rho + 3), rho, 1, "near")
    far = split(project([tok2], *weights))
    cot1, cot3 = gather_near(cot0, "cot")
    far_sum = sum_hop(far, take(far, rho + 3), rho, 1, "far")
    near_sum, own_sum = tie(near_sum, own_sum)
    near_sum = sum_hop(near, near_sum, rho, 2, "near")
    back0 = split(by_slab(back_block, [cot0], w_down, w_down_other, hidden_width))
    cot2 = gather_far(cot1, cot3, "cot")
    far_sum, near_sum, back0 = tie(far_sum, near_sum, back0)
    far_sum = sum_hop(far, far_sum, rho, 2, "far")
    near_sum = sum_hop(near, near_sum, rho, 3, "near")
    far_sum = sum_hop(far, far_sum, rho, 3, "far")
    sums = jnp.concatenate([own_sum, near_sum[:1], far_sum, near_sum[1:]], axis=0)
    gate_sum, up_sum = sums[..., :hidden_width], sums[..., hidden_width:]

    sigmoid = jax.nn.sigmoid(gate_sum)
    silu = gate_sum * sigmoid
    hidden = [narrow(silu * up_sum)]
    back = split(by_slab(back_block, [cot1, cot2, cot3], w_down, w_down_other, hidden_width))
    back = jnp.concatenate([back0, back], axis=0)
    hidden_grad = take(back, rho + 3)
    for step in range(1, RING):
        hidden.append(ring_shift(hidden[-1], f"hidden_{step}"))
        hidden_grad = sum_hop(back, hidden_grad, rho, step, "back")
    hidden = assemble(hidden, rho).reshape(RING * RING * half, hidden_width)
    pre_gate = [narrow(hidden_grad * up_sum * sigmoid * (1.0 + gate_sum * (1.0 - sigmoid)))]
    pre_up = [narrow(hidden_grad * silu)]
    pre_gate.append(ring_shift(pre_gate[0], "pre_gate_1"))
    pre_up.append(ring_shift(pre_up[0], "pre_up_1"))

    slabs = [hidden[i * RING * half : (i + 1) * RING * half] for i in range(RING)]
    mixed = by_slab(down_block, slabs, w_down, w_down_other, CORES * features)
    mixed, pre_gate[1] = tie(mixed, pre_gate[1])
    mixed = mixed.reshape(RING, RING * half, CORES * features)
    for step in range(2, RING):
        pre_gate.append(ring_shift(pre_gate[-1], f"pre_gate_{step}"))
        pre_up.append(ring_shift(pre_up[-1], f"pre_up_{step}"))
    slab = narrow(sum_second(mixed))
    slab = slab.reshape(RING, half, CORES * features)
    block = wide(slab[0])
    for by in (1, 3, 2):
        block = block + wide(first_shift(slab[by], by, f"mixed_first_{by}"))
    block = narrow(block)
    other = swap_cores(block[:, features:], "mixed_swap")
    mixed = jnp.zeros((CORES, half, features), jnp.bfloat16)
    mixed = lax.dynamic_update_slice_in_dim(mixed, block[None, :, :features], core, axis=0)
    mixed = lax.dynamic_update_slice_in_dim(mixed, other[None], 1 - core, axis=0)
    mixed = mixed.reshape(rows, features)

    cot = jnp.concatenate([cot0, cot1, cot2, cot3], axis=0)
    all_tokens = jnp.concatenate([tok0, tok1, tok2, tok3], axis=0)

    def weight_grad(left, right):
        return dot(left, right, ((0,), (0,)))

    hidden, pre_up[1] = tie(hidden, pre_up[1])
    sent = swap_cores(narrow(weight_grad(hidden, cot[:, features:])), "grad_down_swap")
    grad_down = narrow(weight_grad(hidden, cot[:, :features]) + wide(sent))
    grad_down, pre_gate[3] = tie(grad_down, pre_gate[3])

    pre_gate = assemble(pre_gate, rho).reshape(hidden.shape)
    gate_sent = narrow(weight_grad(all_tokens[:, features:], pre_gate))
    gate_sent, pre_up[3] = tie(gate_sent, pre_up[3])
    gate_sent = swap_cores(gate_sent, "grad_gate_swap")
    pre_up = assemble(pre_up, rho).reshape(hidden.shape)
    up_sent = narrow(weight_grad(all_tokens[:, features:], pre_up))
    gate_sent, up_sent = tie(gate_sent, up_sent)
    up_sent = swap_cores(up_sent, "grad_up_swap")
    grad_gate = narrow(weight_grad(all_tokens[:, :features], pre_gate) + wide(gate_sent))
    grad_up = narrow(weight_grad(all_tokens[:, :features], pre_up) + wide(up_sent))
    return mixed, grad_gate, grad_up, grad_down


def solution(mesh):
    return jax.shard_map(
        local,
        mesh=mesh,
        in_specs=(
            P("row", "col"),
            P("col", "row"),
            P("col", "row"),
            P("row", "col"),
            P("row", "col"),
        ),
        out_specs=(P("row", "col"), P("col", "row"), P("col", "row"), P("row", "col")),
        check_vma=False,
    )
```

```python
import functools

import jax
import jax.numpy as jnp
from jax import lax
from jax.experimental import pallas as pl
from jax.experimental.pallas import tpu as pltpu
from jax.sharding import PartitionSpec as P

RING = 4
CORES = 2
DEPTH_STEPS = 2
AXES = ("row", "col")
LONG = pl.CostEstimate(flops=2 * 10**10, bytes_accessed=1, transcendentals=0)


def place(z, y, x, core):
    return ((z * RING + y) * RING + x) * CORES + core


def permute(value, move, name):
    pairs = []
    for z in range(RING):
        for y in range(RING):
            for x in range(RING):
                for core in range(CORES):
                    target = move(z, y, x, core)
                    pairs.append(
                        (
                            place(z, y, x, core),
                            place(
                                target[0] % RING,
                                target[1] % RING,
                                target[2] % RING,
                                target[3],
                            ),
                        )
                    )
    with jax.named_scope(name):
        return lax.ppermute(value, AXES, pairs)


def swap_cores(value, name):
    return permute(value, lambda z, y, x, core: (z, y, x, 1 - core), name)


def first_shift(value, by, name):
    return permute(
        value,
        lambda z, y, x, core: (z, y + by, x, core) if core == 0 else (z + by, y, x, core),
        name,
    )


def second_shift(value, by, name):
    return permute(
        value,
        lambda z, y, x, core: (z + by, y, x, core) if core == 0 else (z, y + by, x, core),
        name,
    )


def ring_shift(value, name):
    return permute(value, lambda z, y, x, core: (z, y, x + 1 - 2 * core, core), name)


def tie(*values):
    return lax.optimization_barrier(values)


def gather_first(own, name):
    before, after, far = (first_shift(own, by, f"{name}_first_{by}") for by in (1, 3, 2))
    return jnp.concatenate([own, after, far, before], axis=0)


def gather_near(own, name):
    return second_shift(own, 3, f"{name}_near_3"), second_shift(own, 1, f"{name}_near_1")


def gather_far(after, before, name):
    half = before.shape[0] // 2
    return jnp.concatenate(
        [
            second_shift(before[:half], 1, f"{name}_far_1"),
            second_shift(after[half:], 3, f"{name}_far_3"),
        ],
        axis=0,
    )


def sum_second(slabs):
    own, after, far, before = slabs
    half = own.shape[0] // 2
    far_after = second_shift(far[:half], 1, "mixed_far_1")
    far_before = second_shift(far[half:], 3, "mixed_far_3")
    after = jnp.concatenate([narrow(wide(after[:half]) + wide(far_after)), after[half:]], axis=0)
    before = jnp.concatenate([before[:half], narrow(wide(before[half:]) + wide(far_before))], axis=0)
    after = second_shift(after, 1, "mixed_near_1")
    before = second_shift(before, 3, "mixed_near_3")
    return wide(own) + wide(after) + wide(before)


def project_block(count, pairs, *refs):
    own, other = refs[:count], refs[count : 2 * count]
    weights, out_ref, acc = refs[2 * count : -2], refs[-2], refs[-1]
    step = pl.program_id(0)
    left = jnp.concatenate(
        [jnp.concatenate([ref[...] for ref in part], axis=0) for part in (own, other)], axis=1
    )
    width = weights[0].shape[1]
    for pair in range(pairs):
        at = pair * width
        right = jnp.concatenate([weights[2 * pair][...], weights[2 * pair + 1][...]], axis=0)
        term = jnp.dot(left, right, preferred_element_type=jnp.float32)

        @pl.when(step == 0)
        def _():
            acc[:, at : at + width] = term

        @pl.when(step == DEPTH_STEPS - 1)
        def _():
            out_ref[:, at : at + width] = (acc[:, at : at + width] + term).astype(out_ref.dtype)


def in_hbm(weights):
    return [pltpu.with_memory_space_constraint(w, pltpu.HBM) for w in weights]


def project(slabs, *weights):
    count, tokens = len(slabs), slabs[0].shape[0]
    features, width = weights[0].shape
    pairs = len(weights) // 2
    depth = features // DEPTH_STEPS
    own = pl.BlockSpec((tokens, depth), lambda k: (0, k))
    other = pl.BlockSpec((tokens, depth), lambda k: (0, k + DEPTH_STEPS))
    weight = pl.BlockSpec((depth, width), lambda k: (k, 0))
    shape = count * tokens, pairs * width
    return pl.pallas_call(
        functools.partial(project_block, count, pairs),
        grid=(DEPTH_STEPS,),
        in_specs=[own] * count + [other] * count + [weight] * len(weights),
        out_specs=pl.BlockSpec(shape, lambda k: (0, 0)),
        out_shape=jax.ShapeDtypeStruct(shape, jnp.bfloat16),
        scratch_shapes=[pltpu.VMEM(shape, jnp.float32)],
        compiler_params=pltpu.CompilerParams(vmem_limit_bytes=28 * 2**20),
        cost_estimate=LONG,
    )(*slabs, *slabs, *in_hbm(weights))


def down_block(count, *refs):
    own_ref, other_ref, out_ref = refs[count:]
    features = own_ref.shape[1]
    for i in range(count):

        @pl.when(pl.program_id(0) == i)
        def _():
            slab = refs[i][...]
            for at, weight in ((0, own_ref), (features, other_ref)):
                term = jnp.dot(slab, weight[...], preferred_element_type=jnp.float32)
                out_ref[:, at : at + features] = term.astype(out_ref.dtype)


def back_block(count, *refs):
    own_ref, other_ref, out_ref = refs[count:]
    features = own_ref.shape[1]
    dims = (((1,), (1,)), ((), ()))
    for i in range(count):

        @pl.when(pl.program_id(0) == i)
        def _():
            slab = refs[i][...]
            term = lax.dot_general(slab[:, :features], own_ref[...], dims, preferred_element_type=jnp.float32)
            term += lax.dot_general(slab[:, features:], other_ref[...], dims, preferred_element_type=jnp.float32)
            out_ref[...] = term.astype(out_ref.dtype)


def by_slab(block, slabs, own, other, width):
    count, (tokens, depth) = len(slabs), slabs[0].shape
    whole = pl.BlockSpec(own.shape, lambda i: (0, 0))
    return pl.pallas_call(
        functools.partial(block, count),
        grid=(count,),
        in_specs=[pl.BlockSpec((tokens, depth), lambda i: (0, 0))] * count + [whole, whole],
        out_specs=pl.BlockSpec((tokens, width), lambda i: (i, 0)),
        out_shape=jax.ShapeDtypeStruct((count * tokens, width), jnp.bfloat16),
        compiler_params=pltpu.CompilerParams(vmem_limit_bytes=28 * 2**20),
        cost_estimate=LONG,
    )(*slabs, *in_hbm([own, other]))


def wide(value):
    return value.astype(jnp.float32)


def narrow(value):
    return value.astype(jnp.bfloat16)


def dot(left, right, dims):
    return lax.dot_general(left, right, (dims, ((), ())), preferred_element_type=jnp.float32)


def take(partial, index):
    return lax.dynamic_index_in_dim(partial, index % RING, axis=1, keepdims=False)


def sum_hop(partial, moving, rho, step, name):
    moving = ring_shift(narrow(moving), f"{name}_hop{step}")
    return wide(moving) + wide(take(partial, rho + 3 - step))


def assemble(parts, rho):
    slabs, tokens, width = parts[0].shape
    whole = jnp.zeros((slabs, RING, tokens, width), parts[0].dtype)
    for step, part in enumerate(parts):
        whole = lax.dynamic_update_slice_in_dim(
            whole, part[:, None], (rho + RING - step) % RING, axis=1
        )
    return whole


def in_rows(parts):
    rows = parts[0].shape[0]
    whole = jnp.zeros((len(parts) * rows, parts[0].shape[1]), parts[0].dtype)
    for i, part in enumerate(parts):
        whole = lax.dynamic_update_slice_in_dim(whole, part, i * rows, axis=0)
    return whole


def local(tokens, w_gate, w_up, w_down, cotangent):
    col = lax.axis_index("col")
    core, x = col % CORES, col // CORES
    rho = jnp.where(core == 0, x, (RING - x) % RING)
    rows, features = tokens.shape
    half = rows // CORES
    hidden_width = w_gate.shape[1]

    acts = jnp.stack([tokens, cotangent]).reshape(2, CORES, half, features)
    mine = lax.dynamic_index_in_dim(acts, core, axis=1, keepdims=False)
    theirs = lax.dynamic_index_in_dim(acts, 1 - core, axis=1, keepdims=False)
    theirs = swap_cores(theirs, "acts_swap")
    theirs, w_gate_sent, w_up_sent = tie(theirs, w_gate, w_up)
    acts = jnp.concatenate([mine, theirs], axis=2)
    w_gate_other, w_up_other = swap_cores(w_gate_sent, "gate_swap"), swap_cores(w_up_sent, "up_swap")

    def split(partial):
        return partial.reshape(-1, RING, half, partial.shape[-1])

    tok0 = gather_first(acts[0], "tok")
    tok0, w_gate_other, w_up_other, w_down_sent = tie(tok0, w_gate_other, w_up_other, w_down)
    tok1, tok3 = gather_near(tok0, "tok")
    w_down_other = swap_cores(w_down_sent, "down_swap")
    weights = w_gate, w_gate_other, w_up, w_up_other
    own = split(project([tok0], *weights))
    own, w_down_other = tie(own, w_down_other)
    own_sum = sum_hop(own, take(own, rho + 3), rho, 1, "own")
    cot_own, tok1, tok3, own_sum = tie(acts[1], tok1, tok3, own_sum)
    tok2 = gather_far(tok1, tok3, "tok")
    cot0 = gather_first(cot_own, "cot")
    own_sum = sum_hop(own, own_sum, rho, 2, "own")
    near = split(project([tok1, tok3], *weights))
    near, own_sum = tie(near, own_sum)
    own_sum = sum_hop(own, own_sum, rho, 3, "own")
    near_sum = sum_hop(near, take(near, rho + 3), rho, 1, "near")
    far = split(project([tok2], *weights))
    cot1, cot3 = gather_near(cot0, "cot")
    far_sum = sum_hop(far, take(far, rho + 3), rho, 1, "far")
    near_sum, own_sum = tie(near_sum, own_sum)
    near_sum = sum_hop(near, near_sum, rho, 2, "near")
    back0 = split(by_slab(back_block, [cot0], w_down, w_down_other, hidden_width))
    cot2 = gather_far(cot1, cot3, "cot")
    far_sum, near_sum, back0 = tie(far_sum, near_sum, back0)
    far_sum = sum_hop(far, far_sum, rho, 2, "far")
    near_sum = sum_hop(near, near_sum, rho, 3, "near")
    far_sum = sum_hop(far, far_sum, rho, 3, "far")
    sums = jnp.concatenate([own_sum, near_sum[:1], far_sum, near_sum[1:]], axis=0)
    gate_sum, up_sum = sums[..., :hidden_width], sums[..., hidden_width:]

    sigmoid = jax.nn.sigmoid(gate_sum)
    silu = gate_sum * sigmoid
    hidden = [narrow(silu * up_sum)]
    back = split(by_slab(back_block, [cot1, cot2, cot3], w_down, w_down_other, hidden_width))
    back = jnp.concatenate([back0, back], axis=0)
    hidden_grad = take(back, rho + 3)
    for step in range(1, RING):
        hidden.append(ring_shift(hidden[-1], f"hidden_{step}"))
        hidden_grad = sum_hop(back, hidden_grad, rho, step, "back")
    hidden = assemble(hidden, rho).reshape(RING * RING * half, hidden_width)
    pre = [
        narrow(
            jnp.concatenate(
                [
                    hidden_grad * up_sum * sigmoid * (1.0 + gate_sum * (1.0 - sigmoid)),
                    hidden_grad * silu,
                ],
                axis=-1,
            )
        )
    ]
    pre.append(ring_shift(pre[0], "pre_1"))

    slabs = [hidden[i * RING * half : (i + 1) * RING * half] for i in range(RING)]
    mixed = by_slab(down_block, slabs, w_down, w_down_other, CORES * features)
    mixed, pre[1] = tie(mixed, pre[1])
    mixed = mixed.reshape(RING, RING * half, CORES * features)
    def weight_grad(left, right):
        return dot(left, right, ((0,), (0,)))

    cot = jnp.concatenate([cot0, cot1, cot2, cot3], axis=0)
    hidden, pre[0] = tie(hidden, pre[0])
    sent = swap_cores(narrow(weight_grad(hidden, cot[:, features:])), "grad_down_swap")
    grad_down = narrow(weight_grad(hidden, cot[:, :features]) + wide(sent))
    pre.append(ring_shift(pre[1], "pre_2"))
    grad_down, pre[2] = tie(grad_down, pre[2])
    pre.append(ring_shift(pre[2], "pre_3"))
    slab = narrow(sum_second(mixed))
    slab = slab.reshape(RING, half, CORES * features)

    token_slabs = jnp.stack([tok0, tok1, tok2, tok3]).reshape(RING, RING, half, CORES * features)
    quarters = [
        take(token_slabs, rho + RING - step).reshape(RING * half, CORES * features)
        for step in range(RING)
    ]

    firsts = [first_shift(slab[by], by, f"mixed_first_{by}") for by in (1, 3, 2)]

    pre = [part.reshape(RING * half, 2 * hidden_width) for part in pre]
    early_tokens, early_pre = in_rows(quarters[:3]), in_rows(pre[:3])
    last_tokens, last_pre = quarters[3], pre[3]
    own, other = slice(0, features), slice(features, CORES * features)
    gate, up = slice(0, hidden_width), slice(hidden_width, 2 * hidden_width)
    early = {
        (side, part): weight_grad(early_tokens[:, columns], early_pre[:, which])
        for side, columns in (("other", other), ("own", own))
        for part, which in (("gate", gate), ("up", up))
    }

    early, last_pre = tie(early, last_pre)

    def whole(side, part):
        columns = own if side == "own" else other
        which = gate if part == "gate" else up
        return early[side, part] + weight_grad(last_tokens[:, columns], last_pre[:, which])

    gate_sent = swap_cores(narrow(whole("other", "gate")), "grad_gate_swap")
    up_sent = swap_cores(narrow(whole("other", "up")), "grad_up_swap")
    grad_gate = narrow(whole("own", "gate") + wide(gate_sent))
    grad_up = narrow(whole("own", "up") + wide(up_sent))
    slab, grad_gate, grad_up = tie(slab, grad_gate, grad_up)
    block = wide(slab[0])
    for first in firsts:
        block = block + wide(first)
    block = narrow(block)
    other = swap_cores(block[:, features:], "mixed_swap")
    mixed = jnp.zeros((CORES, half, features), jnp.bfloat16)
    mixed = lax.dynamic_update_slice_in_dim(mixed, block[None, :, :features], core, axis=0)
    mixed = lax.dynamic_update_slice_in_dim(mixed, other[None], 1 - core, axis=0)
    mixed = mixed.reshape(rows, features)
    return mixed, grad_gate, grad_up, grad_down


def solution(mesh):
    return jax.shard_map(
        local,
        mesh=mesh,
        in_specs=(
            P("row", "col"),
            P("col", "row"),
            P("col", "row"),
            P("row", "col"),
            P("row", "col"),
        ),
        out_specs=(P("row", "col"), P("col", "row"), P("col", "row"), P("row", "col")),
        check_vma=False,
    )
```

```python
import functools

import jax
import jax.numpy as jnp
from jax import lax
from jax.experimental import pallas as pl
from jax.experimental.pallas import tpu as pltpu
from jax.sharding import PartitionSpec as P

RING = 4
CORES = 2
DEPTH_STEPS = 2
AXES = ("row", "col")
LONG = pl.CostEstimate(flops=2 * 10**10, bytes_accessed=1, transcendentals=0)


def place(z, y, x, core):
    return ((z * RING + y) * RING + x) * CORES + core


def permute(value, move, name):
    pairs = []
    for z in range(RING):
        for y in range(RING):
            for x in range(RING):
                for core in range(CORES):
                    target = move(z, y, x, core)
                    pairs.append(
                        (
                            place(z, y, x, core),
                            place(
                                target[0] % RING,
                                target[1] % RING,
                                target[2] % RING,
                                target[3],
                            ),
                        )
                    )
    with jax.named_scope(name):
        return lax.ppermute(value, AXES, pairs)


def swap_cores(value, name):
    return permute(value, lambda z, y, x, core: (z, y, x, 1 - core), name)


def first_shift(value, by, name):
    return permute(
        value,
        lambda z, y, x, core: (z, y + by, x, core) if core == 0 else (z + by, y, x, core),
        name,
    )


def second_shift(value, by, name):
    return permute(
        value,
        lambda z, y, x, core: (z + by, y, x, core) if core == 0 else (z, y + by, x, core),
        name,
    )


def ring_shift(value, name):
    return permute(value, lambda z, y, x, core: (z, y, x + 1 - 2 * core, core), name)


def tie(*values):
    return lax.optimization_barrier(values)


def gather_first(own, name):
    before, after, far = (first_shift(own, by, f"{name}_first_{by}") for by in (1, 3, 2))
    return jnp.concatenate([own, after, far, before], axis=0)


def gather_near(own, name):
    return second_shift(own, 3, f"{name}_near_3"), second_shift(own, 1, f"{name}_near_1")


def gather_far(after, before, name):
    half = before.shape[0] // 2
    return jnp.concatenate(
        [
            second_shift(before[:half], 1, f"{name}_far_1"),
            second_shift(after[half:], 3, f"{name}_far_3"),
        ],
        axis=0,
    )


def sum_second(slabs):
    total = wide(slabs[0])
    for by in (1, 3, 2):
        total = total + wide(second_shift(slabs[by], by, f"mixed_second_{by}"))
    return total


def project_block(count, pairs, *refs):
    own, other = refs[:count], refs[count : 2 * count]
    weights, out_ref, acc = refs[2 * count : -2], refs[-2], refs[-1]
    step = pl.program_id(0)
    left = jnp.concatenate(
        [jnp.concatenate([ref[...] for ref in part], axis=0) for part in (own, other)], axis=1
    )
    width = weights[0].shape[1]
    for pair in range(pairs):
        at = pair * width
        right = jnp.concatenate([weights[2 * pair][...], weights[2 * pair + 1][...]], axis=0)
        term = jnp.dot(left, right, preferred_element_type=jnp.float32)

        @pl.when(step == 0)
        def _():
            acc[:, at : at + width] = term

        @pl.when(step == DEPTH_STEPS - 1)
        def _():
            out_ref[:, at : at + width] = (acc[:, at : at + width] + term).astype(out_ref.dtype)


def in_hbm(weights):
    return [pltpu.with_memory_space_constraint(w, pltpu.HBM) for w in weights]


def project(slabs, *weights):
    count, tokens = len(slabs), slabs[0].shape[0]
    features, width = weights[0].shape
    pairs = len(weights) // 2
    depth = features // DEPTH_STEPS
    own = pl.BlockSpec((tokens, depth), lambda k: (0, k))
    other = pl.BlockSpec((tokens, depth), lambda k: (0, k + DEPTH_STEPS))
    weight = pl.BlockSpec((depth, width), lambda k: (k, 0))
    shape = count * tokens, pairs * width
    return pl.pallas_call(
        functools.partial(project_block, count, pairs),
        grid=(DEPTH_STEPS,),
        in_specs=[own] * count + [other] * count + [weight] * len(weights),
        out_specs=pl.BlockSpec(shape, lambda k: (0, 0)),
        out_shape=jax.ShapeDtypeStruct(shape, jnp.bfloat16),
        scratch_shapes=[pltpu.VMEM(shape, jnp.float32)],
        compiler_params=pltpu.CompilerParams(vmem_limit_bytes=28 * 2**20),
        cost_estimate=LONG,
    )(*slabs, *slabs, *in_hbm(weights))


def down_block(count, *refs):
    own_ref, other_ref, out_ref = refs[count:]
    features = own_ref.shape[1]
    for i in range(count):

        @pl.when(pl.program_id(0) == i)
        def _():
            slab = refs[i][...]
            for at, weight in ((0, own_ref), (features, other_ref)):
                term = jnp.dot(slab, weight[...], preferred_element_type=jnp.float32)
                out_ref[:, at : at + features] = term.astype(out_ref.dtype)


def back_block(count, *refs):
    own_ref, other_ref, out_ref = refs[count:]
    features = own_ref.shape[1]
    dims = (((1,), (1,)), ((), ()))
    for i in range(count):

        @pl.when(pl.program_id(0) == i)
        def _():
            slab = refs[i][...]
            term = lax.dot_general(slab[:, :features], own_ref[...], dims, preferred_element_type=jnp.float32)
            term += lax.dot_general(slab[:, features:], other_ref[...], dims, preferred_element_type=jnp.float32)
            out_ref[...] = term.astype(out_ref.dtype)


def by_slab(block, slabs, own, other, width):
    count, (tokens, depth) = len(slabs), slabs[0].shape
    whole = pl.BlockSpec(own.shape, lambda i: (0, 0))
    return pl.pallas_call(
        functools.partial(block, count),
        grid=(count,),
        in_specs=[pl.BlockSpec((tokens, depth), lambda i: (0, 0))] * count + [whole, whole],
        out_specs=pl.BlockSpec((tokens, width), lambda i: (i, 0)),
        out_shape=jax.ShapeDtypeStruct((count * tokens, width), jnp.bfloat16),
        compiler_params=pltpu.CompilerParams(vmem_limit_bytes=28 * 2**20),
        cost_estimate=LONG,
    )(*slabs, *in_hbm([own, other]))


def wide(value):
    return value.astype(jnp.float32)


def narrow(value):
    return value.astype(jnp.bfloat16)


def dot(left, right, dims):
    return lax.dot_general(left, right, (dims, ((), ())), preferred_element_type=jnp.float32)


def take(partial, index):
    return lax.dynamic_index_in_dim(partial, index % RING, axis=1, keepdims=False)


def sum_hop(partial, moving, rho, step, name):
    moving = ring_shift(narrow(moving), f"{name}_hop{step}")
    return wide(moving) + wide(take(partial, rho + 3 - step))


def assemble(parts, rho):
    slabs, tokens, width = parts[0].shape
    whole = jnp.zeros((slabs, RING, tokens, width), parts[0].dtype)
    for step, part in enumerate(parts):
        whole = lax.dynamic_update_slice_in_dim(
            whole, part[:, None], (rho + RING - step) % RING, axis=1
        )
    return whole


def in_rows(parts):
    rows = parts[0].shape[0]
    whole = jnp.zeros((len(parts) * rows, parts[0].shape[1]), parts[0].dtype)
    for i, part in enumerate(parts):
        whole = lax.dynamic_update_slice_in_dim(whole, part, i * rows, axis=0)
    return whole


def local(tokens, w_gate, w_up, w_down, cotangent):
    col = lax.axis_index("col")
    core, x = col % CORES, col // CORES
    rho = jnp.where(core == 0, x, (RING - x) % RING)
    rows, features = tokens.shape
    half = rows // CORES
    hidden_width = w_gate.shape[1]

    acts = jnp.stack([tokens, cotangent]).reshape(2, CORES, half, features)
    mine = lax.dynamic_index_in_dim(acts, core, axis=1, keepdims=False)
    theirs = lax.dynamic_index_in_dim(acts, 1 - core, axis=1, keepdims=False)
    theirs = swap_cores(theirs, "acts_swap")
    theirs, w_gate_sent, w_up_sent = tie(theirs, w_gate, w_up)
    acts = jnp.concatenate([mine, theirs], axis=2)
    w_gate_other, w_up_other = swap_cores(w_gate_sent, "gate_swap"), swap_cores(w_up_sent, "up_swap")

    def split(partial):
        return partial.reshape(-1, RING, half, partial.shape[-1])

    tok0 = gather_first(acts[0], "tok")
    tok0, w_gate_other, w_up_other, w_down_sent = tie(tok0, w_gate_other, w_up_other, w_down)
    tok1, tok3 = gather_near(tok0, "tok")
    w_down_other = swap_cores(w_down_sent, "down_swap")
    weights = w_gate, w_gate_other, w_up, w_up_other
    own = split(project([tok0], *weights))
    own, w_down_other = tie(own, w_down_other)
    own_sum = sum_hop(own, take(own, rho + 3), rho, 1, "own")
    cot_own, tok1, tok3, own_sum = tie(acts[1], tok1, tok3, own_sum)
    tok2 = gather_far(tok1, tok3, "tok")
    cot0 = gather_first(cot_own, "cot")
    own_sum = sum_hop(own, own_sum, rho, 2, "own")
    tok1, tok3, own_sum = tie(tok1, tok3, own_sum)
    near = split(project([tok1, tok3], *weights))
    own_sum = sum_hop(own, own_sum, rho, 3, "own")
    near_sum = sum_hop(near, take(near, rho + 3), rho, 1, "near")
    far = split(project([tok2], *weights))
    cot1, cot3 = gather_near(cot0, "cot")
    far_sum = sum_hop(far, take(far, rho + 3), rho, 1, "far")
    near_sum, own_sum = tie(near_sum, own_sum)
    near_sum = sum_hop(near, near_sum, rho, 2, "near")
    back0 = split(by_slab(back_block, [cot0], w_down, w_down_other, hidden_width))
    cot2 = gather_far(cot1, cot3, "cot")
    far_sum, near_sum, back0 = tie(far_sum, near_sum, back0)
    far_sum = sum_hop(far, far_sum, rho, 2, "far")
    near_sum = sum_hop(near, near_sum, rho, 3, "near")
    far_sum = sum_hop(far, far_sum, rho, 3, "far")
    sums = jnp.concatenate([own_sum, near_sum[:1], far_sum, near_sum[1:]], axis=0)
    gate_sum, up_sum = sums[..., :hidden_width], sums[..., hidden_width:]

    sigmoid = jax.nn.sigmoid(gate_sum)
    silu = gate_sum * sigmoid
    hidden = [narrow(silu * up_sum)]
    back = split(by_slab(back_block, [cot1, cot2, cot3], w_down, w_down_other, hidden_width))
    back = jnp.concatenate([back0, back], axis=0)
    hidden_grad = take(back, rho + 3)
    for step in range(1, RING):
        hidden.append(ring_shift(hidden[-1], f"hidden_{step}"))
        hidden_grad = sum_hop(back, hidden_grad, rho, step, "back")
    hidden = assemble(hidden, rho).reshape(RING * RING * half, hidden_width)
    pre = [
        narrow(
            jnp.concatenate(
                [
                    hidden_grad * up_sum * sigmoid * (1.0 + gate_sum * (1.0 - sigmoid)),
                    hidden_grad * silu,
                ],
                axis=-1,
            )
        )
    ]
    pre.append(ring_shift(pre[0], "pre_1"))

    slabs = [hidden[i * RING * half : (i + 1) * RING * half] for i in range(RING)]
    mixed = by_slab(down_block, slabs, w_down, w_down_other, CORES * features)
    mixed, pre[1] = tie(mixed, pre[1])
    mixed = mixed.reshape(RING, RING * half, CORES * features)
    def weight_grad(left, right):
        return dot(left, right, ((0,), (0,)))

    cot = jnp.concatenate([cot0, cot1, cot2, cot3], axis=0)
    hidden, pre[0] = tie(hidden, pre[0])
    sent = swap_cores(narrow(weight_grad(hidden, cot[:, features:])), "grad_down_swap")
    grad_down = narrow(weight_grad(hidden, cot[:, :features]) + wide(sent))
    pre.append(ring_shift(pre[1], "pre_2"))
    grad_down, pre[2] = tie(grad_down, pre[2])
    pre.append(ring_shift(pre[2], "pre_3"))
    slab = narrow(sum_second(mixed))
    slab = slab.reshape(RING, half, CORES * features)

    token_slabs = jnp.stack([tok0, tok1, tok2, tok3]).reshape(RING, RING, half, CORES * features)
    quarters = [
        take(token_slabs, rho + RING - step).reshape(RING * half, CORES * features)
        for step in range(RING)
    ]

    firsts = [first_shift(slab[by], by, f"mixed_first_{by}") for by in (1, 3, 2)]

    pre = [part.reshape(RING * half, 2 * hidden_width) for part in pre]
    early_tokens, early_pre = in_rows(quarters[:3]), in_rows(pre[:3])
    last_tokens, last_pre = quarters[3], pre[3]
    own, other = slice(0, features), slice(features, CORES * features)
    gate, up = slice(0, hidden_width), slice(hidden_width, 2 * hidden_width)
    early = {
        (side, part): weight_grad(early_tokens[:, columns], early_pre[:, which])
        for side, columns in (("other", other), ("own", own))
        for part, which in (("gate", gate), ("up", up))
    }

    early, last_pre = tie(early, last_pre)

    def whole(side, part):
        columns = own if side == "own" else other
        which = gate if part == "gate" else up
        return early[side, part] + weight_grad(last_tokens[:, columns], last_pre[:, which])

    gate_sent = swap_cores(narrow(whole("other", "gate")), "grad_gate_swap")
    up_sent = swap_cores(narrow(whole("other", "up")), "grad_up_swap")
    grad_gate = narrow(whole("own", "gate") + wide(gate_sent))
    grad_up = narrow(whole("own", "up") + wide(up_sent))
    slab, grad_gate, grad_up = tie(slab, grad_gate, grad_up)
    block = wide(slab[0])
    for first in firsts:
        block = block + wide(first)
    block = narrow(block)
    other = swap_cores(block[:, features:], "mixed_swap")
    mixed = jnp.zeros((CORES, half, features), jnp.bfloat16)
    mixed = lax.dynamic_update_slice_in_dim(mixed, block[None, :, :features], core, axis=0)
    mixed = lax.dynamic_update_slice_in_dim(mixed, other[None], 1 - core, axis=0)
    mixed = mixed.reshape(rows, features)
    return mixed, grad_gate, grad_up, grad_down


def solution(mesh):
    return jax.shard_map(
        local,
        mesh=mesh,
        in_specs=(
            P("row", "col"),
            P("col", "row"),
            P("col", "row"),
            P("row", "col"),
            P("row", "col"),
        ),
        out_specs=(P("row", "col"), P("col", "row"), P("col", "row"), P("row", "col")),
        check_vma=False,
    )
```

```python
import functools

import jax
import jax.numpy as jnp
from jax import lax
from jax.experimental import pallas as pl
from jax.experimental.pallas import tpu as pltpu
from jax.sharding import PartitionSpec as P

RING = 4
CORES = 2
DEPTH_STEPS = 2
AXES = ("row", "col")
LONG = pl.CostEstimate(flops=2 * 10**10, bytes_accessed=1, transcendentals=0)


def place(z, y, x, core):
    return ((z * RING + y) * RING + x) * CORES + core


def permute(value, move, name):
    pairs = []
    for z in range(RING):
        for y in range(RING):
            for x in range(RING):
                for core in range(CORES):
                    target = move(z, y, x, core)
                    pairs.append(
                        (
                            place(z, y, x, core),
                            place(
                                target[0] % RING,
                                target[1] % RING,
                                target[2] % RING,
                                target[3],
                            ),
                        )
                    )
    with jax.named_scope(name):
        return lax.ppermute(value, AXES, pairs)


def swap_cores(value, name):
    return permute(value, lambda z, y, x, core: (z, y, x, 1 - core), name)


def first_shift(value, by, name):
    return permute(
        value,
        lambda z, y, x, core: (z, y + by, x, core) if core == 0 else (z + by, y, x, core),
        name,
    )


def second_shift(value, by, name):
    return permute(
        value,
        lambda z, y, x, core: (z + by, y, x, core) if core == 0 else (z, y + by, x, core),
        name,
    )


def ring_shift(value, name):
    return permute(value, lambda z, y, x, core: (z, y, x + 1 - 2 * core, core), name)


def tie(*values):
    return lax.optimization_barrier(values)


def gather_first(own, name):
    before, after, far = (first_shift(own, by, f"{name}_first_{by}") for by in (1, 3, 2))
    return jnp.concatenate([own, after, far, before], axis=0)


def gather_near(own, name):
    return second_shift(own, 3, f"{name}_near_3"), second_shift(own, 1, f"{name}_near_1")


def gather_far(after, before, name):
    half = before.shape[0] // 2
    return jnp.concatenate(
        [
            second_shift(before[:half], 1, f"{name}_far_1"),
            second_shift(after[half:], 3, f"{name}_far_3"),
        ],
        axis=0,
    )


def sum_second(slabs):
    total = wide(slabs[0])
    for by in (1, 3, 2):
        total = total + wide(second_shift(slabs[by], by, f"mixed_second_{by}"))
    return total


def project_block(count, pairs, *refs):
    own, other = refs[:count], refs[count : 2 * count]
    weights, out_ref, acc = refs[2 * count : -2], refs[-2], refs[-1]
    step = pl.program_id(0)
    left = jnp.concatenate(
        [jnp.concatenate([ref[...] for ref in part], axis=0) for part in (own, other)], axis=1
    )
    width = weights[0].shape[1]
    for pair in range(pairs):
        at = pair * width
        right = jnp.concatenate([weights[2 * pair][...], weights[2 * pair + 1][...]], axis=0)
        term = jnp.dot(left, right, preferred_element_type=jnp.float32)

        @pl.when(step == 0)
        def _():
            acc[:, at : at + width] = term

        @pl.when(step == DEPTH_STEPS - 1)
        def _():
            out_ref[:, at : at + width] = (acc[:, at : at + width] + term).astype(out_ref.dtype)


def in_hbm(weights):
    return [pltpu.with_memory_space_constraint(w, pltpu.HBM) for w in weights]


def project(slabs, *weights):
    count, tokens = len(slabs), slabs[0].shape[0]
    features, width = weights[0].shape
    pairs = len(weights) // 2
    depth = features // DEPTH_STEPS
    own = pl.BlockSpec((tokens, depth), lambda k: (0, k))
    other = pl.BlockSpec((tokens, depth), lambda k: (0, k + DEPTH_STEPS))
    weight = pl.BlockSpec((depth, width), lambda k: (k, 0))
    shape = count * tokens, pairs * width
    return pl.pallas_call(
        functools.partial(project_block, count, pairs),
        grid=(DEPTH_STEPS,),
        in_specs=[own] * count + [other] * count + [weight] * len(weights),
        out_specs=pl.BlockSpec(shape, lambda k: (0, 0)),
        out_shape=jax.ShapeDtypeStruct(shape, jnp.bfloat16),
        scratch_shapes=[pltpu.VMEM(shape, jnp.float32)],
        compiler_params=pltpu.CompilerParams(vmem_limit_bytes=28 * 2**20),
        cost_estimate=LONG,
    )(*slabs, *slabs, *in_hbm(weights))


def down_block(count, *refs):
    own_ref, other_ref, out_ref = refs[count:]
    features = own_ref.shape[1]
    for i in range(count):

        @pl.when(pl.program_id(0) == i)
        def _():
            slab = refs[i][...]
            for at, weight in ((0, own_ref), (features, other_ref)):
                term = jnp.dot(slab, weight[...], preferred_element_type=jnp.float32)
                out_ref[:, at : at + features] = term.astype(out_ref.dtype)


def back_block(count, *refs):
    own_ref, other_ref, out_ref = refs[count:]
    features = own_ref.shape[1]
    dims = (((1,), (1,)), ((), ()))
    for i in range(count):

        @pl.when(pl.program_id(0) == i)
        def _():
            slab = refs[i][...]
            term = lax.dot_general(slab[:, :features], own_ref[...], dims, preferred_element_type=jnp.float32)
            term += lax.dot_general(slab[:, features:], other_ref[...], dims, preferred_element_type=jnp.float32)
            out_ref[...] = term.astype(out_ref.dtype)


def by_slab(block, slabs, own, other, width):
    count, (tokens, depth) = len(slabs), slabs[0].shape
    whole = pl.BlockSpec(own.shape, lambda i: (0, 0))
    return pl.pallas_call(
        functools.partial(block, count),
        grid=(count,),
        in_specs=[pl.BlockSpec((tokens, depth), lambda i: (0, 0))] * count + [whole, whole],
        out_specs=pl.BlockSpec((tokens, width), lambda i: (i, 0)),
        out_shape=jax.ShapeDtypeStruct((count * tokens, width), jnp.bfloat16),
        compiler_params=pltpu.CompilerParams(vmem_limit_bytes=28 * 2**20),
        cost_estimate=LONG,
    )(*slabs, *in_hbm([own, other]))


def wide(value):
    return value.astype(jnp.float32)


def narrow(value):
    return value.astype(jnp.bfloat16)


def dot(left, right, dims):
    return lax.dot_general(left, right, (dims, ((), ())), preferred_element_type=jnp.float32)


def take(partial, index):
    return lax.dynamic_index_in_dim(partial, index % RING, axis=1, keepdims=False)


def sum_hop(partial, moving, rho, step, name):
    moving = ring_shift(narrow(moving), f"{name}_hop{step}")
    return wide(moving) + wide(take(partial, rho + 3 - step))


def assemble(parts, rho):
    slabs, tokens, width = parts[0].shape
    whole = jnp.zeros((slabs, RING, tokens, width), parts[0].dtype)
    for step, part in enumerate(parts):
        whole = lax.dynamic_update_slice_in_dim(
            whole, part[:, None], (rho + RING - step) % RING, axis=1
        )
    return whole


def in_rows(parts):
    rows = parts[0].shape[0]
    whole = jnp.zeros((len(parts) * rows, parts[0].shape[1]), parts[0].dtype)
    for i, part in enumerate(parts):
        whole = lax.dynamic_update_slice_in_dim(whole, part, i * rows, axis=0)
    return whole


def local(tokens, w_gate, w_up, w_down, cotangent):
    col = lax.axis_index("col")
    core, x = col % CORES, col // CORES
    rho = jnp.where(core == 0, x, (RING - x) % RING)
    rows, features = tokens.shape
    half = rows // CORES
    hidden_width = w_gate.shape[1]

    acts = jnp.stack([tokens, cotangent]).reshape(2, CORES, half, features)
    mine = lax.dynamic_index_in_dim(acts, core, axis=1, keepdims=False)
    theirs = lax.dynamic_index_in_dim(acts, 1 - core, axis=1, keepdims=False)
    theirs = swap_cores(theirs, "acts_swap")
    theirs, w_gate_sent, w_up_sent = tie(theirs, w_gate, w_up)
    acts = jnp.concatenate([mine, theirs], axis=2)
    w_gate_other, w_up_other = swap_cores(w_gate_sent, "gate_swap"), swap_cores(w_up_sent, "up_swap")

    def split(partial):
        return partial.reshape(-1, RING, half, partial.shape[-1])

    tok0 = gather_first(acts[0], "tok")
    tok0, w_gate_other, w_up_other, w_down_sent = tie(tok0, w_gate_other, w_up_other, w_down)
    tok1, tok3 = gather_near(tok0, "tok")
    w_down_other = swap_cores(w_down_sent, "down_swap")
    weights = w_gate, w_gate_other, w_up, w_up_other
    own = split(project([tok0], *weights))
    own, w_down_other = tie(own, w_down_other)
    own_sum = sum_hop(own, take(own, rho + 3), rho, 1, "own")
    cot_own, tok1, tok3, own_sum = tie(acts[1], tok1, tok3, own_sum)
    tok2 = gather_far(tok1, tok3, "tok")
    cot0 = gather_first(cot_own, "cot")
    own_sum = sum_hop(own, own_sum, rho, 2, "own")
    tok1, tok3, own_sum = tie(tok1, tok3, own_sum)
    near = split(project([tok1, tok3], *weights))
    own_sum = sum_hop(own, own_sum, rho, 3, "own")
    near_sum = sum_hop(near, take(near, rho + 3), rho, 1, "near")
    far = split(project([tok2], *weights))
    cot3, cot1, cot2 = (second_shift(cot0, by, f"cot_second_{by}") for by in (1, 3, 2))
    far_sum = sum_hop(far, take(far, rho + 3), rho, 1, "far")
    near_sum, own_sum = tie(near_sum, own_sum)
    near_sum = sum_hop(near, near_sum, rho, 2, "near")
    back0 = split(by_slab(back_block, [cot0], w_down, w_down_other, hidden_width))
    far_sum, near_sum, back0 = tie(far_sum, near_sum, back0)
    far_sum = sum_hop(far, far_sum, rho, 2, "far")
    far_sum, cot1, cot2, cot3 = tie(far_sum, cot1, cot2, cot3)
    near_sum = sum_hop(near, near_sum, rho, 3, "near")
    far_sum = sum_hop(far, far_sum, rho, 3, "far")
    sums = jnp.concatenate([own_sum, near_sum[:1], far_sum, near_sum[1:]], axis=0)
    gate_sum, up_sum = sums[..., :hidden_width], sums[..., hidden_width:]

    sigmoid = jax.nn.sigmoid(gate_sum)
    silu = gate_sum * sigmoid
    hidden = [narrow(silu * up_sum)]
    back = split(by_slab(back_block, [cot1, cot2, cot3], w_down, w_down_other, hidden_width))
    back = jnp.concatenate([back0, back], axis=0)
    hidden_grad = take(back, rho + 3)
    for step in range(1, RING):
        hidden.append(ring_shift(hidden[-1], f"hidden_{step}"))
        hidden_grad = sum_hop(back, hidden_grad, rho, step, "back")
    hidden = assemble(hidden, rho).reshape(RING * RING * half, hidden_width)
    pre = [
        narrow(
            jnp.concatenate(
                [
                    hidden_grad * up_sum * sigmoid * (1.0 + gate_sum * (1.0 - sigmoid)),
                    hidden_grad * silu,
                ],
                axis=-1,
            )
        )
    ]
    pre.append(ring_shift(pre[0], "pre_1"))

    slabs = [hidden[i * RING * half : (i + 1) * RING * half] for i in range(RING)]
    mixed = by_slab(down_block, slabs, w_down, w_down_other, CORES * features)
    mixed, pre[1] = tie(mixed, pre[1])
    mixed = mixed.reshape(RING, RING * half, CORES * features)
    def weight_grad(left, right):
        return dot(left, right, ((0,), (0,)))

    cot = jnp.concatenate([cot0, cot1, cot2, cot3], axis=0)
    hidden, pre[0] = tie(hidden, pre[0])
    sent = swap_cores(narrow(weight_grad(hidden, cot[:, features:])), "grad_down_swap")
    grad_down = narrow(weight_grad(hidden, cot[:, :features]) + wide(sent))
    pre.append(ring_shift(pre[1], "pre_2"))
    grad_down, pre[2] = tie(grad_down, pre[2])
    pre.append(ring_shift(pre[2], "pre_3"))
    slab = narrow(sum_second(mixed))
    slab = slab.reshape(RING, half, CORES * features)

    token_slabs = jnp.stack([tok0, tok1, tok2, tok3]).reshape(RING, RING, half, CORES * features)
    quarters = [
        take(token_slabs, rho + RING - step).reshape(RING * half, CORES * features)
        for step in range(RING)
    ]

    firsts = [first_shift(slab[by], by, f"mixed_first_{by}") for by in (1, 3, 2)]

    pre = [part.reshape(RING * half, 2 * hidden_width) for part in pre]
    early_tokens, early_pre = in_rows(quarters[:3]), in_rows(pre[:3])
    last_tokens, last_pre = quarters[3], pre[3]
    own, other = slice(0, features), slice(features, CORES * features)
    gate, up = slice(0, hidden_width), slice(hidden_width, 2 * hidden_width)
    early = {
        (side, part): weight_grad(early_tokens[:, columns], early_pre[:, which])
        for side, columns in (("other", other), ("own", own))
        for part, which in (("gate", gate), ("up", up))
    }

    early, last_pre = tie(early, last_pre)

    def whole(side, part):
        columns = own if side == "own" else other
        which = gate if part == "gate" else up
        return early[side, part] + weight_grad(last_tokens[:, columns], last_pre[:, which])

    gate_sent = swap_cores(narrow(whole("other", "gate")), "grad_gate_swap")
    up_sent = swap_cores(narrow(whole("other", "up")), "grad_up_swap")
    grad_gate = narrow(whole("own", "gate") + wide(gate_sent))
    grad_up = narrow(whole("own", "up") + wide(up_sent))
    slab, grad_gate, grad_up = tie(slab, grad_gate, grad_up)
    block = wide(slab[0])
    for first in firsts:
        block = block + wide(first)
    block = narrow(block)
    other = swap_cores(block[:, features:], "mixed_swap")
    mixed = jnp.zeros((CORES, half, features), jnp.bfloat16)
    mixed = lax.dynamic_update_slice_in_dim(mixed, block[None, :, :features], core, axis=0)
    mixed = lax.dynamic_update_slice_in_dim(mixed, other[None], 1 - core, axis=0)
    mixed = mixed.reshape(rows, features)
    return mixed, grad_gate, grad_up, grad_down


def solution(mesh):
    return jax.shard_map(
        local,
        mesh=mesh,
        in_specs=(
            P("row", "col"),
            P("col", "row"),
            P("col", "row"),
            P("row", "col"),
            P("row", "col"),
        ),
        out_specs=(P("row", "col"), P("col", "row"), P("col", "row"), P("row", "col")),
        check_vma=False,
    )
```
